32 devices in a mesh: seq: 4 (over y, x), dp: 8 (over z, core).
Axes of the slice: x: 2, y: 2, z: 4, core: 2. Of those that a mesh axis runs over, the one named last changes fastest.
Arguments:
- frames: bfloat16 [16, 512, 3072], P('dp', 'seq'), may hold values from -6 to 6
- proj_weight: bfloat16 [3072, 4608], P('dp'), may hold values from -0.109375 to 0.109375
- rate_weight: bfloat16 [3072, 24], replicated, may hold values from -0.109375 to 0.109375
- rate_bias: float32 [24], replicated, may hold values from -2 to 1
- init_weights: float32 [2, 24, 64, 256], replicated, may hold values from -0.75 to 0.75
- init_bias_hidden: float32 [24, 256], replicated, may hold values from -3 to 3
- init_bias_out: float32 [24, 64], replicated, may hold values from -3 to 3
- out_gain: float32 [1536], replicated, may hold values from 0.5 to 1.5
Outputs:
- ttt_output: bfloat16 [16, 512, 1536], P('dp', 'seq')
The draws below stay inside these ranges and needn't reach their ends.
All inputs are finite; a program needn't handle non-finite values.
Results may differ from the reference program's by a relative error of at most 0.0091.
Values may be sent and summed in bfloat16 or wider, within the bound.
A program may use at most 128 MiB of HBM per device.

```python
import math
import jax
import jax.numpy as jnp
from jax import lax

D = 3072
H = 24
HD = 64
HF = 256
MB = 64
SLAB = 128
HH = 1536
SEQLEN = 512
NCLIPS = 16
N_SEQ = 4


def block_scale(stream_key, dims, split, smallest, top_value):
    level, own = 1.0, jax.random.fold_in(stream_key, 6)
    for axis_at, parts in split:
        draws = jnp.exp(jax.random.uniform(jax.random.fold_in(own, axis_at), (parts,), jnp.float32, smallest / len(split), top_value / len(split)))
        level = level * jnp.repeat(draws, dims[axis_at] // parts).reshape([-1 if axis == axis_at else 1 for axis in range(len(dims))])
    return level


def noise(own_key, shape, spread, reach, shards=(), kind=jnp.bfloat16):
    level = block_scale(own_key, shape, shards, -0.22, 0.18) if shards else 1.0
    values = jax.random.normal(own_key, shape, jnp.float32) * spread * level
    return jnp.minimum(jnp.maximum(values, -reach), reach).astype(kind)


def setup_inputs(seed: int = 0) -> dict:
    arg_keys = jax.random.split(jax.random.key(seed), 9)
    return {
        "frames": noise(arg_keys[0], (NCLIPS, SEQLEN, D), 1.0, 6.0, ((0, 8), (1, 4))),
        "proj_weight": noise(arg_keys[1], (D, 3 * HH), D ** -0.5, 0.109375, ((0, 8),)),
        "rate_weight": noise(arg_keys[2], (D, H), D ** -0.5, 0.109375),
        "rate_bias": jnp.clip(jax.random.uniform(arg_keys[3], (H,), jnp.float32, -2.0, 1.0), -2.0, 1.0),
        "init_weights": noise(arg_keys[4], (2, H, HD, HF), HD ** -0.5, 0.75, (), jnp.float32),
        "init_bias_hidden": noise(arg_keys[5], (H, HF), 0.5, 3.0, (), jnp.float32),
        "init_bias_out": noise(arg_keys[6], (H, HD), 0.5, 3.0, (), jnp.float32),
        "out_gain": jnp.clip(1.0 + 0.1 * jax.random.normal(arg_keys[7], (HH,), jnp.float32), 0.5, 1.5),
    }


precise = lax.Precision.HIGHEST
coefficient = 0.044715
root_scale = math.sqrt(2.0 / math.pi)

def gelu_pair(z_value):
    tanh_part = jnp.tanh(root_scale * (z_value + coefficient * z_value * z_value * z_value))
    result = 0.5 * z_value * (1.0 + tanh_part)
    derivative = 0.5 * (1.0 + tanh_part) + 0.5 * z_value * (1.0 - tanh_part * tanh_part) * root_scale * (1.0 + 3.0 * coefficient * z_value * z_value)
    return (result, derivative)

def minibatch(carried, inputs):
    pair, bias_hidden, bias_out = carried
    queries, key_rows, values, step_rate = inputs
    w_first = pair[0]
    w_second = pair[1]
    block_len = queries.shape[1]
    causal = jnp.tril(jnp.ones((block_len, block_len), dtype=bool))
    z_first = jnp.einsum('hbd,hdf->hbf', key_rows, w_first, precision=precise) + bias_hidden[:, None, :]
    hidden, derivative = gelu_pair(z_first)
    z_second = jnp.einsum('hbf,hdf->hbd', hidden, w_second, precision=precise) + bias_out[:, None, :]
    grad_second = z_second - (values - key_rows)
    grad_first = jnp.einsum('hbd,hdf->hbf', grad_second, w_second, precision=precise) * derivative
    scores_first = jnp.einsum('htd,hsd->hts', queries, key_rows, precision=precise) + 1.0
    mix_first = jnp.where(causal[None], scores_first * step_rate[:, None, :], 0.0)
    zq_first = jnp.einsum('htd,hdf->htf', queries, w_first, precision=precise) + bias_hidden[:, None, :]
    zq_first = zq_first - jnp.einsum('hts,hsf->htf', mix_first, grad_first, precision=precise)
    hidden_query, unused = gelu_pair(zq_first)
    scores_second = jnp.einsum('htf,hsf->hts', hidden_query, hidden, precision=precise) + 1.0
    mix_second = jnp.where(causal[None], scores_second * step_rate[:, None, :], 0.0)
    zq_second = jnp.einsum('htf,hdf->htd', hidden_query, w_second, precision=precise) + bias_out[:, None, :]
    zq_second = zq_second - jnp.einsum('hts,hsd->htd', mix_second, grad_second, precision=precise)
    scaled_first = grad_first * step_rate[:, :, None]
    scaled_second = grad_second * step_rate[:, :, None]
    new_first = w_first - jnp.einsum('hbd,hbf->hdf', key_rows, scaled_first, precision=precise)
    new_second = w_second - jnp.einsum('hbd,hbf->hdf', scaled_second, hidden, precision=precise)
    new_pair = jnp.stack([new_first, new_second])
    new_hidden = bias_hidden - lax.optimization_barrier(jnp.sum(scaled_first, axis=1))
    new_out = bias_out - lax.optimization_barrier(jnp.sum(scaled_second, axis=1))
    return ((new_pair, new_hidden, new_out), queries + zq_second)

def one_slab(carried, slab_inputs):
    final_state, results = lax.scan(minibatch, carried, slab_inputs)
    final_state = jax.tree.map(lambda member: lax.optimization_barrier(member.astype(jnp.bfloat16)).astype(jnp.float32), final_state)
    return (final_state, results)

def reference(frames, proj_weight, rate_weight, rate_bias, init_weights, init_bias_hidden, init_bias_out, out_gain):
    gain_rows = out_gain.reshape(H, HD)
    batches = SLAB // MB

    def one_clip(clip_frames):
        projected = jnp.dot(clip_frames, proj_weight, preferred_element_type=jnp.float32).astype(jnp.bfloat16)
        projected = projected.reshape(SEQLEN, 3, H, HD)
        rates = jax.nn.sigmoid(jnp.dot(clip_frames, rate_weight, preferred_element_type=jnp.float32) + rate_bias) / (MB * (HD + HF))
        inputs = projected.astype(jnp.float32).reshape(N_SEQ, batches, MB, 3, H, HD).transpose(3, 0, 1, 4, 2, 5)
        step_rate = rates.reshape(N_SEQ, batches, MB, H).transpose(0, 1, 3, 2)
        start_state = (init_weights, init_bias_hidden, init_bias_out)
        unused, results = lax.scan(one_slab, start_state, (inputs[0], inputs[1], inputs[2], step_rate))
        results = results.transpose(0, 1, 3, 2, 4).reshape(SEQLEN, H, HD)
        normed = results * lax.rsqrt(lax.optimization_barrier(jnp.mean(results * results, axis=-1, keepdims=True)) + 1e-06) * gain_rows
        return normed.reshape(SEQLEN, H * HD).astype(jnp.bfloat16)
    return lax.map(one_clip, frames)
```

```python
import functools
import math

import jax
import jax.numpy as jnp
from jax import lax
from jax.experimental import pallas as pl
from jax.experimental.pallas import tpu as pltpu
from jax.sharding import PartitionSpec as P

MB = 64
PAIR = 2
coefficient = 0.044715
root_scale = math.sqrt(2.0 / math.pi)
f32 = jnp.float32
bf16 = jnp.bfloat16


def gelu_value(z):
    u = z * z
    t = jnp.tanh(z * (root_scale + (root_scale * coefficient) * u))
    h = 0.5 * z
    return h + h * t


def gelu_pair(z):
    u = z * z
    t = jnp.tanh(z * (root_scale + (root_scale * coefficient) * u))
    h = 0.5 * z
    value = h + h * t
    slope = (0.5 + 0.5 * t) + h * (1.0 - t * t) * (
        root_scale + (3.0 * root_scale * coefficient) * u
    )
    return value, slope


def dot(a, b):
    return jnp.dot(a, b, preferred_element_type=f32)


def dot_t(a, b):
    return lax.dot_general(a, b, (((1,), (1,)), ((), ())), preferred_element_type=f32)


def block_masks(width, step):
    rows = lax.broadcasted_iota(jnp.int32, (width, width), 0)
    cols = lax.broadcasted_iota(jnp.int32, (width, width), 1)
    same = (rows // step) == (cols // step)
    return same, same & (cols <= rows)


def ttt_step(read, state, rate_row, gain_row, masks, blocks):
    same, causal = masks
    w1_ref, b1_ref, w2_ref, b2_ref = state
    step = MB
    width = blocks * step
    q, k, v = read
    zero = jnp.zeros((), bf16)
    k_bd = jnp.where(same, jnp.concatenate([k] * blocks, axis=0), zero)
    q_bd = jnp.where(same, jnp.concatenate([q] * blocks, axis=0), zero)
    w1 = w1_ref[...]
    w2 = w2_ref[...]
    w1_low = w1.astype(bf16)
    w2_low = w2.astype(bf16)
    b1 = b1_ref[...]
    b2 = b2_ref[0:1, :]
    b1_rows = jnp.concatenate(
        [jnp.broadcast_to(b1[i : i + 1], (step, b1.shape[1])) for i in range(blocks)], axis=0
    )
    z1 = dot(k_bd, w1_low) + b1_rows
    x2, slope = gelu_pair(z1)
    x2_low = x2.astype(bf16)
    target = b2 - (v.astype(f32) - k.astype(f32))
    z2 = dot_t(x2_low, w2_low)
    g2 = jnp.where(same, z2 + jnp.concatenate([target] * blocks, axis=0), 0.0)
    g2_low = g2.astype(bf16)
    g1_low = (dot(g2_low, w2_low) * slope).astype(bf16)
    m1 = jnp.where(causal, (dot_t(q_bd, k_bd) + 1.0) * rate_row, 0.0).astype(bf16)
    z1q = dot(q_bd, w1_low) + b1_rows - dot(m1, g1_low)
    x2q_low = gelu_value(z1q).astype(bf16)
    m2 = jnp.where(causal, (dot_t(x2q_low, x2_low) + 1.0) * rate_row, 0.0).astype(bf16)
    z2q = dot_t(x2q_low, w2_low) - dot(m2, g2_low)
    lane = lax.broadcasted_iota(jnp.int32, (step, width), 1) // step
    out = z2q[:step]
    for i in range(1, blocks):
        out = jnp.where(lane == i, z2q[i * step : (i + 1) * step], out)
    y = q.astype(f32) + out + b2
    member = lax.broadcasted_iota(jnp.int32, (8, width), 0)
    rate_bd = jnp.where(
        member == lax.broadcasted_iota(jnp.int32, (8, width), 1) // step, rate_row, 0.0
    ).astype(bf16)
    k_scaled = (k_bd.astype(f32).T * rate_row).astype(bf16)
    g2_scaled = (g2.T * rate_row).astype(bf16)
    w1_ref[...] = w1 - dot(k_scaled, g1_low)
    b1_ref[...] = b1 - dot(rate_bd, g1_low)
    w2_ref[...] = w2 - dot(g2_scaled, x2_low)
    db2 = dot(rate_bd, g2_low)
    b2_ref[0:1, :] = b2 - jnp.sum(db2, axis=0, keepdims=True)
    square = dot((y * y).astype(bf16), same.astype(bf16)) * (1.0 / step)
    return y * lax.rsqrt(square + 1e-06) * gain_row


def round_state(state):
    for ref in state:
        ref[...] = ref[...].astype(bf16).astype(f32)


def ttt_kernel(groups, clips, proj_ref, rate_ref, w1_in, b1_in, w2_in, b2_in, gain_ref, out_ref, *scratch):
    blocks = clips * PAIR
    slabs = proj_ref.shape[0]
    batches = proj_ref.shape[2] // MB
    lanes = PAIR * MB
    states = [scratch[4 * g : 4 * g + 4] for g in range(groups)]
    for g in range(groups):
        for c in range(clips):
            states[g][0][c * lanes : (c + 1) * lanes, :] = w1_in[g]
            states[g][2][c * lanes : (c + 1) * lanes, :] = w2_in[g]
        states[g][1][...] = b1_in[g]
        states[g][3][...] = b2_in[g]

    def slab_body(s, carry):
        masks = block_masks(blocks * MB, MB)
        for b in range(batches):
            for g in range(groups):
                read = [
                    jnp.concatenate(
                        [
                            proj_ref[s, c, b * MB : (b + 1) * MB, (3 * g + part) * lanes : (3 * g + part + 1) * lanes]
                            for c in range(clips)
                        ],
                        axis=1,
                    )
                    for part in range(3)
                ]
                y = ttt_step(
                    read, states[g], rate_ref[g, s * batches + b], gain_ref[g], masks, blocks
                ).astype(bf16)
                for c in range(clips):
                    out_ref[s, c, b * MB : (b + 1) * MB, g * lanes : (g + 1) * lanes] = y[
                        :, c * lanes : (c + 1) * lanes
                    ]
        for g in range(groups):
            round_state(states[g])
        return carry

    lax.fori_loop(0, slabs, slab_body, 0)


def on_device(
    frames,
    proj_weight,
    rate_weight,
    rate_bias,
    init_weights,
    init_bias_hidden,
    init_bias_out,
    out_gain,
):
    clips, slab_len, model_width = frames.shape
    heads = rate_weight.shape[1]
    size = init_weights.shape[2]
    inner = init_weights.shape[3]
    length = lax.axis_size("seq")
    position = lax.axis_index("seq")
    mine = heads // length
    groups = -(-mine // PAIR)
    padded = groups * PAIR
    lanes = PAIR * size
    blocks = clips * PAIR
    batches = slab_len // MB
    first = position * mine

    def own(array, axis):
        part = lax.dynamic_slice_in_dim(array, first, mine, axis)
        pads = [(0, 0)] * array.ndim
        pads[axis] = (0, padded - mine)
        return jnp.pad(part, pads) if padded > mine else part

    weight = own(proj_weight.reshape(-1, 3, heads, size), 2)
    weight = weight.reshape(-1, 3, groups, lanes).transpose(0, 2, 1, 3).reshape(-1, groups * 3 * lanes)
    weight = lax.all_gather(weight, "dp", axis=0, tiled=True)
    all_frames = lax.all_gather(frames, "seq", axis=0)
    rows = all_frames.reshape(length * clips * slab_len, model_width)
    projected = jnp.dot(rows, weight, preferred_element_type=f32).astype(bf16)
    projected = projected.reshape(length, clips, slab_len, groups * 3 * lanes)
    rates = jnp.dot(rows, own(rate_weight, 1), preferred_element_type=f32)
    rates = jax.nn.sigmoid(rates + own(rate_bias, 0)) / (MB * (size + inner))
    rates = rates.reshape(length, clips, batches, MB, groups, PAIR).transpose(4, 0, 2, 1, 5, 3)
    rates = rates.reshape(groups, length * batches, 1, blocks * MB)
    w_own = own(init_weights, 1).reshape(2, groups, lanes, inner)
    b1 = own(init_bias_hidden, 0).reshape(groups, 1, PAIR, inner)
    b1 = jnp.broadcast_to(b1, (groups, clips, PAIR, inner)).reshape(groups, blocks, inner)
    b1 = jnp.pad(b1, ((0, 0), (0, 8 - blocks), (0, 0)))
    b2 = own(init_bias_out, 0).reshape(groups, 1, 1, lanes)
    b2 = jnp.broadcast_to(b2, (groups, 8, clips, lanes)).reshape(groups, 8, blocks * size)
    gain = own(out_gain.reshape(heads, size), 0).reshape(groups, 1, 1, lanes)
    gain = jnp.broadcast_to(gain, (groups, 1, clips, lanes)).reshape(groups, 1, blocks * size)

    results = pl.pallas_call(
        functools.partial(ttt_kernel, groups, clips),
        out_shape=jax.ShapeDtypeStruct((length, clips, slab_len, groups * lanes), bf16),
        in_specs=[pl.BlockSpec(memory_space=pltpu.VMEM)] * 7,
        out_specs=pl.BlockSpec(memory_space=pltpu.VMEM),
        scratch_shapes=[
            pltpu.VMEM((blocks * size, inner), f32),
            pltpu.VMEM((8, inner), f32),
            pltpu.VMEM((blocks * size, inner), f32),
            pltpu.VMEM((8, blocks * size), f32),
        ]
        * groups,
        compiler_params=pltpu.CompilerParams(vmem_limit_bytes=48 * 1024 * 1024),
        name="fast_state",
    )(projected, rates, w_own[0], b1, w_own[1], b2, gain)

    exchanged = lax.all_to_all(results, "seq", 0, 0)
    exchanged = exchanged[..., : mine * size]
    return exchanged.transpose(1, 2, 0, 3).reshape(clips, slab_len, heads * size)


def solution(mesh):
    return jax.shard_map(
        on_device,
        mesh=mesh,
        in_specs=(P("dp", "seq", None), P("dp", None), P(), P(), P(), P(), P(), P()),
        out_specs=P("dp", "seq", None),
        check_vma=False,
    )
```

```python
import functools
import math

import jax
import jax.numpy as jnp
from jax import lax
from jax.experimental import pallas as pl
from jax.experimental.pallas import tpu as pltpu
from jax.sharding import PartitionSpec as P

MB = 64
PAIR = 2
coefficient = 0.044715
root_scale = math.sqrt(2.0 / math.pi)
f32 = jnp.float32
bf16 = jnp.bfloat16


def gelu_value(z):
    u = z * z
    t = jnp.tanh(z * (root_scale + (root_scale * coefficient) * u))
    h = 0.5 * z
    return h + h * t


def gelu_pair(z):
    u = z * z
    t = jnp.tanh(z * (root_scale + (root_scale * coefficient) * u))
    h = 0.5 * z
    value = h + h * t
    slope = (0.5 + 0.5 * t) + h * (1.0 - t * t) * (
        root_scale + (3.0 * root_scale * coefficient) * u
    )
    return value, slope


def dot(a, b):
    return jnp.dot(a, b, preferred_element_type=f32)


def dot_t(a, b):
    return lax.dot_general(a, b, (((1,), (1,)), ((), ())), preferred_element_type=f32)


def block_masks(width, step):
    rows = lax.broadcasted_iota(jnp.int32, (width, width), 0)
    cols = lax.broadcasted_iota(jnp.int32, (width, width), 1)
    same = (rows // step) == (cols // step)
    return same, same & (cols <= rows)


def ttt_step(read, state, rate_row, gain_row, masks, blocks):
    same, causal = masks
    w1_ref, b1_ref, w2_ref, b2_ref = state
    step = MB
    width = blocks * step
    q, k, v = read
    zero = jnp.zeros((), bf16)
    k_bd = jnp.where(same, jnp.concatenate([k] * blocks, axis=0), zero)
    q_bd = jnp.where(same, jnp.concatenate([q] * blocks, axis=0), zero)
    w1 = w1_ref[...]
    w2 = w2_ref[...]
    w1_low = w1.astype(bf16)
    w2_low = w2.astype(bf16)
    b1 = b1_ref[...]
    b2 = b2_ref[0:1, :]
    b1_rows = jnp.concatenate(
        [jnp.broadcast_to(b1[i : i + 1], (step, b1.shape[1])) for i in range(blocks)], axis=0
    )
    z1 = dot(k_bd, w1_low) + b1_rows
    x2, slope = gelu_pair(z1)
    x2_low = x2.astype(bf16)
    target = b2 - (v.astype(f32) - k.astype(f32))
    z2 = dot_t(x2_low, w2_low)
    g2 = jnp.where(same, z2 + jnp.concatenate([target] * blocks, axis=0), 0.0)
    g2_low = g2.astype(bf16)
    g1_low = (dot(g2_low, w2_low) * slope).astype(bf16)
    m1 = jnp.where(causal, (dot_t(q_bd, k_bd) + 1.0) * rate_row, 0.0).astype(bf16)
    z1q = dot(q_bd, w1_low) + b1_rows - dot(m1, g1_low)
    x2q_low = gelu_value(z1q).astype(bf16)
    m2 = jnp.where(causal, (dot_t(x2q_low, x2_low) + 1.0) * rate_row, 0.0).astype(bf16)
    z2q = dot_t(x2q_low, w2_low) - dot(m2, g2_low)
    lane = lax.broadcasted_iota(jnp.int32, (step, width), 1) // step
    out = z2q[:step]
    for i in range(1, blocks):
        out = jnp.where(lane == i, z2q[i * step : (i + 1) * step], out)
    y = q.astype(f32) + out + b2
    member = lax.broadcasted_iota(jnp.int32, (8, width), 0)
    rate_bd = jnp.where(
        member == lax.broadcasted_iota(jnp.int32, (8, width), 1) // step, rate_row, 0.0
    ).astype(bf16)
    k_scaled = (k_bd.astype(f32).T * rate_row).astype(bf16)
    g2_scaled = (g2.T * rate_row).astype(bf16)
    w1_ref[...] = w1 - dot(k_scaled, g1_low)
    b1_ref[...] = b1 - dot(rate_bd, g1_low)
    w2_ref[...] = w2 - dot(g2_scaled, x2_low)
    db2 = dot(rate_bd, g2_low)
    b2_ref[0:1, :] = b2 - jnp.sum(db2, axis=0, keepdims=True)
    square = dot((y * y).astype(bf16), same.astype(bf16)) * (1.0 / step)
    return y * lax.rsqrt(square + 1e-06) * gain_row


def round_state(state):
    for ref in state:
        ref[...] = ref[...].astype(bf16).astype(f32)


def ttt_kernel(groups, clips, proj_ref, rate_ref, w1_in, b1_in, w2_in, b2_in, gain_ref, out_ref, *scratch):
    blocks = clips * PAIR
    slabs = proj_ref.shape[0]
    batches = proj_ref.shape[2] // MB
    lanes = PAIR * MB
    states = [scratch[4 * g : 4 * g + 4] for g in range(groups)]
    for g in range(groups):
        for c in range(clips):
            states[g][0][c * lanes : (c + 1) * lanes, :] = w1_in[g]
            states[g][2][c * lanes : (c + 1) * lanes, :] = w2_in[g]
        states[g][1][...] = b1_in[g]
        states[g][3][...] = b2_in[g]

    def slab_body(s, carry):
        masks = block_masks(blocks * MB, MB)
        for b in range(batches):
            for g in range(groups):
                read = [
                    jnp.concatenate(
                        [
                            proj_ref[s, c, b * MB : (b + 1) * MB, (part * groups + g) * lanes : (part * groups + g + 1) * lanes]
                            for c in range(clips)
                        ],
                        axis=1,
                    )
                    for part in range(3)
                ]
                y = ttt_step(
                    read, states[g], rate_ref[g, s * batches + b], gain_ref[g], masks, blocks
                ).astype(bf16)
                for c in range(clips):
                    out_ref[s, c, b * MB : (b + 1) * MB, g * lanes : (g + 1) * lanes] = y[
                        :, c * lanes : (c + 1) * lanes
                    ]
        for g in range(groups):
            round_state(states[g])
        return carry

    lax.fori_loop(0, slabs, slab_body, 0)


def gather_kernel(
    n_seq, n_dp, f_ref, w_ref, f_all, w_all, f_send, f_recv, w_send, w_recv, own_sem
):
    seq, dp = lax.axis_index("seq"), lax.axis_index("dp")
    a, b = seq // 2, lax.rem(seq, 2)
    z, c = dp // 2, lax.rem(dp, 2)
    n_a, n_c = n_seq // 2, n_dp // 2
    peers = [lax.rem(a + i, n_a) * 2 + b for i in range(1, n_a)]
    pair = a * 2 + 1 - b
    sibling = z * 2 + 1 - c
    has_right, has_left = z + 1 < n_c, z > 0

    own_f = pltpu.make_async_copy(f_ref, f_all.at[seq], own_sem.at[0])
    own_w = pltpu.make_async_copy(w_ref, w_all.at[dp], own_sem.at[1])
    own_f.start()
    own_w.start()

    barrier = pltpu.get_barrier_semaphore()
    for other in peers + [pair]:
        pl.semaphore_signal(
            barrier, inc=1, device_id={"seq": other}, device_id_type=pl.DeviceIdType.MESH
        )
    pl.semaphore_signal(
        barrier, inc=1, device_id={"dp": sibling}, device_id_type=pl.DeviceIdType.MESH
    )

    @pl.when(has_right)
    def _():
        pl.semaphore_signal(
            barrier, inc=1, device_id={"dp": dp + 2}, device_id_type=pl.DeviceIdType.MESH
        )

    @pl.when(has_left)
    def _():
        pl.semaphore_signal(
            barrier, inc=1, device_id={"dp": dp - 2}, device_id_type=pl.DeviceIdType.MESH
        )

    neighbours = jnp.where(has_right, 1, 0) + jnp.where(has_left, 1, 0)
    pl.semaphore_wait(barrier, neighbours + (len(peers) + 2))

    pending = []

    def send_f(source, owner, half, to):
        copy = pltpu.make_async_remote_copy(
            source,
            f_all.at[owner, half],
            f_send.at[len(pending)],
            f_recv.at[owner, half],
            device_id={"seq": to},
            device_id_type=pl.DeviceIdType.MESH,
        )
        copy.start()
        pending.append(copy)

    def got_f(owner, half):
        pltpu.make_async_remote_copy(
            f_all.at[owner, half],
            f_all.at[owner, half],
            f_send.at[0],
            f_recv.at[owner, half],
            device_id={"seq": pair},
            device_id_type=pl.DeviceIdType.MESH,
        ).wait_recv()

    def copy_w(source, owner, piece, way, distance):
        to = (dp + 2, dp - 2, sibling)[way]
        return pltpu.make_async_remote_copy(
            source,
            w_all.at[owner, piece],
            w_send.at[(way * n_c + distance) * 2 + piece],
            w_recv.at[owner, piece],
            device_id={"dp": to},
            device_id_type=pl.DeviceIdType.MESH,
        )

    def got_w(owner, piece):
        copy_w(w_all.at[owner, piece], owner, piece, 2, 0).wait_recv()

    for piece in range(2):

        @pl.when(has_right)
        def _():
            copy_w(w_ref.at[piece], dp, piece, 0, 0).start()

        @pl.when(has_left)
        def _():
            copy_w(w_ref.at[piece], dp, piece, 1, 0).start()

    for half in (0, 1):
        for other in peers:
            send_f(f_ref.at[half], seq, half, other)
        send_f(f_ref.at[1 - half], seq, 1 - half, pair)
    for piece in range(2):
        copy_w(w_ref.at[piece], dp, piece, 2, 0).start()

    for distance in range(1, n_c):
        for piece in range(2):
            for way, sign, here, onward in (
                (0, -1, z >= distance, has_right),
                (1, 1, z + distance < n_c, has_left),
            ):
                owner = dp + sign * 2 * distance

                @pl.when(here)
                def _():
                    got_w(owner, piece)

                    @pl.when(onward)
                    def _():
                        copy_w(w_all.at[owner, piece], owner, piece, way, distance).start()

                    share(w_all, w_send, w_recv, owner, piece, way, distance, n_c, sibling).start()

            if distance == 1 and piece == 0:
                relay_f(peers, pair, got_f, send_f, f_all)
    if n_c == 1:
        relay_f(peers, pair, got_f, send_f, f_all)

    for other in peers:
        got_f(other, 1)
        far = other + 1 - 2 * b
        got_f(far, 0)
        got_f(far, 1)
    got_f(pair, 0)
    for chip in range(n_c):
        for piece in range(2):
            got_w(chip * 2 + 1 - c, piece)

    for copy in pending:
        copy.wait_send()
    for piece in range(2):

        @pl.when(has_right)
        def _():
            copy_w(w_ref.at[piece], dp, piece, 0, 0).wait_send()

        @pl.when(has_left)
        def _():
            copy_w(w_ref.at[piece], dp, piece, 1, 0).wait_send()

        copy_w(w_ref.at[piece], dp, piece, 2, 0).wait_send()
        for distance in range(1, n_c):
            for way, sign, here, onward in (
                (0, -1, z >= distance, has_right),
                (1, 1, z + distance < n_c, has_left),
            ):
                owner = dp + sign * 2 * distance

                @pl.when(here)
                def _():
                    @pl.when(onward)
                    def _():
                        copy_w(w_all.at[owner, piece], owner, piece, way, distance).wait_send()

                    share(
                        w_all, w_send, w_recv, owner, piece, way, distance, n_c, sibling
                    ).wait_send()

    own_f.wait()
    own_w.wait()


def relay_f(peers, pair, got_f, send_f, f_all):
    for other in peers:
        got_f(other, 0)
        send_f(f_all.at[other, 0], other, 0, pair)
    got_f(pair, 1)
    for other in peers:
        send_f(f_all.at[pair, 1], pair, 1, other)


def share(w_all, w_send, w_recv, owner, piece, way, distance, n_c, sibling):
    return pltpu.make_async_remote_copy(
        w_all.at[owner, piece],
        w_all.at[owner, piece],
        w_send.at[((2 + way) * n_c + distance) * 2 + piece],
        w_recv.at[owner, piece],
        device_id={"dp": sibling},
        device_id_type=pl.DeviceIdType.MESH,
    )


def gather_both(frames, weight, n_seq, n_dp):
    clips, slab_len, width = frames.shape
    depth, columns = weight.shape
    n_a, n_c = n_seq // 2, n_dp // 2
    halves = frames.reshape(2, clips * slab_len // 2, width)
    pieces = weight.reshape(2, depth // 2, columns)
    f_all, w_all = pl.pallas_call(
        functools.partial(gather_kernel, n_seq, n_dp),
        out_shape=(
            jax.ShapeDtypeStruct((n_seq,) + halves.shape, bf16),
            jax.ShapeDtypeStruct((n_dp,) + pieces.shape, bf16),
        ),
        in_specs=[pl.BlockSpec(memory_space=pl.ANY)] * 2,
        out_specs=(pl.BlockSpec(memory_space=pl.ANY),) * 2,
        scratch_shapes=[
            pltpu.SemaphoreType.DMA((2 * n_a + 2 * (n_a - 1),)),
            pltpu.SemaphoreType.DMA((n_seq, 2)),
            pltpu.SemaphoreType.DMA((4 * n_c * 2,)),
            pltpu.SemaphoreType.DMA((n_dp, 2)),
            pltpu.SemaphoreType.DMA((2,)),
        ],
        compiler_params=pltpu.CompilerParams(collective_id=0, has_side_effects=True),
        name="gather_both",
    )(halves, pieces)
    return f_all.reshape(n_seq * clips * slab_len, width), w_all.reshape(n_dp * depth, columns)


def on_device(
    frames,
    proj_weight,
    rate_weight,
    rate_bias,
    init_weights,
    init_bias_hidden,
    init_bias_out,
    out_gain,
):
    clips, slab_len, model_width = frames.shape
    heads = rate_weight.shape[1]
    size = init_weights.shape[2]
    inner = init_weights.shape[3]
    length = lax.axis_size("seq")
    position = lax.axis_index("seq")
    mine = heads // length
    groups = -(-mine // PAIR)
    padded = groups * PAIR
    lanes = PAIR * size
    blocks = clips * PAIR
    batches = slab_len // MB
    first = position * mine

    def own(array, axis):
        part = lax.dynamic_slice_in_dim(array, first, mine, axis)
        pads = [(0, 0)] * array.ndim
        pads[axis] = (0, padded - mine)
        return jnp.pad(part, pads) if padded > mine else part

    span = proj_weight.shape[1] // 3
    parts = [
        lax.dynamic_slice_in_dim(proj_weight, part * span + first * size, mine * size, 1)
        for part in range(3)
    ]
    if padded > mine:
        parts = [jnp.pad(part, ((0, 0), (0, (padded - mine) * size))) for part in parts]
    weight = jnp.concatenate(parts, axis=1)
    rows, weight = gather_both(frames, weight, length, lax.axis_size("dp"))
    projected = jnp.dot(rows, weight, preferred_element_type=f32).astype(bf16)
    projected = projected.reshape(length, clips, slab_len, groups * 3 * lanes)
    rates = jnp.dot(rows, own(rate_weight, 1), preferred_element_type=f32)
    rates = jax.nn.sigmoid(rates + own(rate_bias, 0)) / (MB * (size + inner))
    rates = rates.reshape(length, clips, batches, MB, groups, PAIR).transpose(4, 0, 2, 1, 5, 3)
    rates = rates.reshape(groups, length * batches, 1, blocks * MB)
    w_own = own(init_weights, 1).reshape(2, groups, lanes, inner)
    b1 = own(init_bias_hidden, 0).reshape(groups, 1, PAIR, inner)
    b1 = jnp.broadcast_to(b1, (groups, clips, PAIR, inner)).reshape(groups, blocks, inner)
    b1 = jnp.pad(b1, ((0, 0), (0, 8 - blocks), (0, 0)))
    b2 = own(init_bias_out, 0).reshape(groups, 1, 1, lanes)
    b2 = jnp.broadcast_to(b2, (groups, 8, clips, lanes)).reshape(groups, 8, blocks * size)
    gain = own(out_gain.reshape(heads, size), 0).reshape(groups, 1, 1, lanes)
    gain = jnp.broadcast_to(gain, (groups, 1, clips, lanes)).reshape(groups, 1, blocks * size)

    results = pl.pallas_call(
        functools.partial(ttt_kernel, groups, clips),
        out_shape=jax.ShapeDtypeStruct((length, clips, slab_len, groups * lanes), bf16),
        in_specs=[pl.BlockSpec(memory_space=pltpu.VMEM)] * 7,
        out_specs=pl.BlockSpec(memory_space=pltpu.VMEM),
        scratch_shapes=[
            pltpu.VMEM((blocks * size, inner), f32),
            pltpu.VMEM((8, inner), f32),
            pltpu.VMEM((blocks * size, inner), f32),
            pltpu.VMEM((8, blocks * size), f32),
        ]
        * groups,
        compiler_params=pltpu.CompilerParams(vmem_limit_bytes=48 * 1024 * 1024),
        name="fast_state",
    )(projected, rates, w_own[0], b1, w_own[1], b2, gain)

    exchanged = lax.all_to_all(results, "seq", 0, 0)
    exchanged = exchanged[..., : mine * size]
    return exchanged.transpose(1, 2, 0, 3).reshape(clips, slab_len, heads * size)


def solution(mesh):
    return jax.shard_map(
        on_device,
        mesh=mesh,
        in_specs=(P("dp", "seq", None), P("dp", None), P(), P(), P(), P(), P(), P()),
        out_specs=P("dp", "seq", None),
        check_vma=False,
    )
```

```python
import functools
import math

import jax
import jax.numpy as jnp
from jax import lax
from jax.experimental import pallas as pl
from jax.experimental.pallas import tpu as pltpu
from jax.sharding import PartitionSpec as P

MB = 64
PAIR = 2
coefficient = 0.044715
root_scale = math.sqrt(2.0 / math.pi)
f32 = jnp.float32
bf16 = jnp.bfloat16


def gelu_value(z):
    u = z * z
    t = jnp.tanh(z * (root_scale + (root_scale * coefficient) * u))
    h = 0.5 * z
    return h + h * t


def gelu_pair(z):
    u = z * z
    t = jnp.tanh(z * (root_scale + (root_scale * coefficient) * u))
    h = 0.5 * z
    value = h + h * t
    slope = (0.5 + 0.5 * t) + h * (1.0 - t * t) * (
        root_scale + (3.0 * root_scale * coefficient) * u
    )
    return value, slope


def dot(a, b):
    return jnp.dot(a, b, preferred_element_type=f32)


def dot_t(a, b):
    return lax.dot_general(a, b, (((1,), (1,)), ((), ())), preferred_element_type=f32)


def block_masks(width, step):
    rows = lax.broadcasted_iota(jnp.int32, (width, width), 0)
    cols = lax.broadcasted_iota(jnp.int32, (width, width), 1)
    same = (rows // step) == (cols // step)
    return same, same & (cols <= rows)


def ttt_step(read, state, rate_row, gain_row, masks, blocks):
    same, causal = masks
    w1_ref, b1_ref, w2_ref, b2_ref = state
    step = MB
    width = blocks * step
    q, k, v = read
    zero = jnp.zeros((), bf16)
    k_bd = jnp.where(same, jnp.concatenate([k] * blocks, axis=0), zero)
    q_bd = jnp.where(same, jnp.concatenate([q] * blocks, axis=0), zero)
    w1 = w1_ref[...]
    w2 = w2_ref[...]
    w1_low = w1.astype(bf16)
    w2_low = w2.astype(bf16)
    b1 = b1_ref[...]
    b2 = b2_ref[0:1, :]
    b1_rows = jnp.concatenate(
        [jnp.broadcast_to(b1[i : i + 1], (step, b1.shape[1])) for i in range(blocks)], axis=0
    )
    z1 = dot(k_bd, w1_low) + b1_rows
    x2, slope = gelu_pair(z1)
    x2_low = x2.astype(bf16)
    target = b2 - (v.astype(f32) - k.astype(f32))
    z2 = dot_t(x2_low, w2_low)
    g2 = jnp.where(same, z2 + jnp.concatenate([target] * blocks, axis=0), 0.0)
    g2_low = g2.astype(bf16)
    g1_low = (dot(g2_low, w2_low) * slope).astype(bf16)
    m1 = jnp.where(causal, (dot_t(q_bd, k_bd) + 1.0) * rate_row, 0.0).astype(bf16)
    z1q = dot(q_bd, w1_low) + b1_rows - dot(m1, g1_low)
    x2q_low = gelu_value(z1q).astype(bf16)
    m2 = jnp.where(causal, (dot_t(x2q_low, x2_low) + 1.0) * rate_row, 0.0).astype(bf16)
    z2q = dot_t(x2q_low, w2_low) - dot(m2, g2_low)
    lane = lax.broadcasted_iota(jnp.int32, (step, width), 1) // step
    out = z2q[:step]
    for i in range(1, blocks):
        out = jnp.where(lane == i, z2q[i * step : (i + 1) * step], out)
    y = q.astype(f32) + out + b2
    member = lax.broadcasted_iota(jnp.int32, (8, width), 0)
    rate_bd = jnp.where(
        member == lax.broadcasted_iota(jnp.int32, (8, width), 1) // step, rate_row, 0.0
    ).astype(bf16)
    k_scaled = (k_bd.astype(f32).T * rate_row).astype(bf16)
    g2_scaled = (g2.T * rate_row).astype(bf16)
    w1_ref[...] = w1 - dot(k_scaled, g1_low)
    b1_ref[...] = b1 - dot(rate_bd, g1_low)
    w2_ref[...] = w2 - dot(g2_scaled, x2_low)
    db2 = dot(rate_bd, g2_low)
    b2_ref[0:1, :] = b2 - jnp.sum(db2, axis=0, keepdims=True)
    square = dot((y * y).astype(bf16), same.astype(bf16)) * (1.0 / step)
    return y * lax.rsqrt(square + 1e-06) * gain_row


def round_state(state):
    for ref in state:
        ref[...] = ref[...].astype(bf16).astype(f32)


def ttt_kernel(groups, clips, proj_ref, rate_ref, w1_in, b1_in, w2_in, b2_in, gain_ref, out_ref, *scratch):
    blocks = clips * PAIR
    slabs = proj_ref.shape[0]
    batches = proj_ref.shape[2] // MB
    lanes = PAIR * MB
    states = [scratch[4 * g : 4 * g + 4] for g in range(groups)]
    for g in range(groups):
        for c in range(clips):
            states[g][0][c * lanes : (c + 1) * lanes, :] = w1_in[g]
            states[g][2][c * lanes : (c + 1) * lanes, :] = w2_in[g]
        states[g][1][...] = b1_in[g]
        states[g][3][...] = b2_in[g]

    def slab_body(s, carry):
        masks = block_masks(blocks * MB, MB)
        for b in range(batches):
            for g in range(groups):
                read = [
                    jnp.concatenate(
                        [
                            proj_ref[s, c, b * MB : (b + 1) * MB, (part * groups + g) * lanes : (part * groups + g + 1) * lanes]
                            for c in range(clips)
                        ],
                        axis=1,
                    )
                    for part in range(3)
                ]
                y = ttt_step(
                    read, states[g], rate_ref[g, s * batches + b], gain_ref[g], masks, blocks
                ).astype(bf16)
                for c in range(clips):
                    out_ref[s, c, b * MB : (b + 1) * MB, g * lanes : (g + 1) * lanes] = y[
                        :, c * lanes : (c + 1) * lanes
                    ]
        for g in range(groups):
            round_state(states[g])
        return carry

    lax.fori_loop(0, slabs, slab_body, 0)


def gather_kernel(
    n_seq, n_dp, f_ref, w_ref, f_all, w_all, f_send, f_recv, w_send, w_recv, own_sem
):
    seq, dp = lax.axis_index("seq"), lax.axis_index("dp")
    a, b = seq // 2, lax.rem(seq, 2)
    z, c = dp // 2, lax.rem(dp, 2)
    n_a, n_c = n_seq // 2, n_dp // 2
    peers = [lax.rem(a + i, n_a) * 2 + b for i in range(1, n_a)]
    pair = a * 2 + 1 - b
    sibling = z * 2 + 1 - c
    has_right, has_left = z + 1 < n_c, z > 0

    own_f = pltpu.make_async_copy(f_ref, f_all.at[seq], own_sem.at[0])
    own_w = pltpu.make_async_copy(w_ref, w_all.at[dp], own_sem.at[1])
    own_f.start()
    own_w.start()

    barrier = pltpu.get_barrier_semaphore()
    for other in peers + [pair]:
        pl.semaphore_signal(
            barrier, inc=1, device_id={"seq": other}, device_id_type=pl.DeviceIdType.MESH
        )
    pl.semaphore_signal(
        barrier, inc=1, device_id={"dp": sibling}, device_id_type=pl.DeviceIdType.MESH
    )

    @pl.when(has_right)
    def _():
        pl.semaphore_signal(
            barrier, inc=1, device_id={"dp": dp + 2}, device_id_type=pl.DeviceIdType.MESH
        )

    @pl.when(has_left)
    def _():
        pl.semaphore_signal(
            barrier, inc=1, device_id={"dp": dp - 2}, device_id_type=pl.DeviceIdType.MESH
        )

    neighbours = jnp.where(has_right, 1, 0) + jnp.where(has_left, 1, 0)
    pl.semaphore_wait(barrier, neighbours + (len(peers) + 2))

    pending = []

    def send_f(source, owner, half, to):
        copy = pltpu.make_async_remote_copy(
            source,
            f_all.at[owner, half],
            f_send.at[len(pending)],
            f_recv.at[owner, half],
            device_id={"seq": to},
            device_id_type=pl.DeviceIdType.MESH,
        )
        copy.start()
        pending.append(copy)

    def got_f(owner, half):
        pltpu.make_async_remote_copy(
            f_all.at[owner, half],
            f_all.at[owner, half],
            f_send.at[0],
            f_recv.at[owner, half],
            device_id={"seq": pair},
            device_id_type=pl.DeviceIdType.MESH,
        ).wait_recv()

    def copy_w(source, owner, piece, way, distance):
        to = (dp + 2, dp - 2, sibling)[way]
        return pltpu.make_async_remote_copy(
            source,
            w_all.at[owner, piece],
            w_send.at[(way * n_c + distance) * 2 + piece],
            w_recv.at[owner, piece],
            device_id={"dp": to},
            device_id_type=pl.DeviceIdType.MESH,
        )

    def got_w(owner, piece):
        copy_w(w_all.at[owner, piece], owner, piece, 2, 0).wait_recv()

    for piece in range(2):

        @pl.when(has_right)
        def _():
            copy_w(w_ref.at[piece], dp, piece, 0, 0).start()

        @pl.when(has_left)
        def _():
            copy_w(w_ref.at[piece], dp, piece, 1, 0).start()

    for half in (0, 1):
        for other in peers:
            send_f(f_ref.at[half], seq, half, other)
        send_f(f_ref.at[1 - half], seq, 1 - half, pair)
    for piece in range(2):
        copy_w(w_ref.at[piece], dp, piece, 2, 0).start()

    for distance in range(1, n_c):
        for piece in range(2):
            for way, sign, here, onward in (
                (0, -1, z >= distance, has_right),
                (1, 1, z + distance < n_c, has_left),
            ):
                owner = dp + sign * 2 * distance

                @pl.when(here)
                def _():
                    got_w(owner, piece)

                    @pl.when(onward)
                    def _():
                        copy_w(w_all.at[owner, piece], owner, piece, way, distance).start()

                    share(w_all, w_send, w_recv, owner, piece, way, distance, n_c, sibling).start()

            if distance == 1 and piece == 1:
                relay_f(peers, pair, got_f, send_f, f_all)
    if n_c == 1:
        relay_f(peers, pair, got_f, send_f, f_all)

    for other in peers:
        got_f(other, 1)
        far = other + 1 - 2 * b
        got_f(far, 0)
        got_f(far, 1)
    got_f(pair, 0)
    for chip in range(n_c):
        for piece in range(2):
            got_w(chip * 2 + 1 - c, piece)

    for copy in pending:
        copy.wait_send()
    for piece in range(2):

        @pl.when(has_right)
        def _():
            copy_w(w_ref.at[piece], dp, piece, 0, 0).wait_send()

        @pl.when(has_left)
        def _():
            copy_w(w_ref.at[piece], dp, piece, 1, 0).wait_send()

        copy_w(w_ref.at[piece], dp, piece, 2, 0).wait_send()
        for distance in range(1, n_c):
            for way, sign, here, onward in (
                (0, -1, z >= distance, has_right),
                (1, 1, z + distance < n_c, has_left),
            ):
                owner = dp + sign * 2 * distance

                @pl.when(here)
                def _():
                    @pl.when(onward)
                    def _():
                        copy_w(w_all.at[owner, piece], owner, piece, way, distance).wait_send()

                    share(
                        w_all, w_send, w_recv, owner, piece, way, distance, n_c, sibling
                    ).wait_send()

    own_f.wait()
    own_w.wait()


def relay_f(peers, pair, got_f, send_f, f_all):
    for other in peers:
        got_f(other, 0)
        send_f(f_all.at[other, 0], other, 0, pair)
    got_f(pair, 1)
    for other in peers:
        send_f(f_all.at[pair, 1], pair, 1, other)


def share(w_all, w_send, w_recv, owner, piece, way, distance, n_c, sibling):
    return pltpu.make_async_remote_copy(
        w_all.at[owner, piece],
        w_all.at[owner, piece],
        w_send.at[((2 + way) * n_c + distance) * 2 + piece],
        w_recv.at[owner, piece],
        device_id={"dp": sibling},
        device_id_type=pl.DeviceIdType.MESH,
    )


def gather_both(frames, weight, n_seq, n_dp):
    clips, slab_len, width = frames.shape
    depth, columns = weight.shape
    n_a, n_c = n_seq // 2, n_dp // 2
    halves = frames.reshape(2, clips * slab_len // 2, width)
    pieces = weight.reshape(2, depth // 2, columns)
    f_all, w_all = pl.pallas_call(
        functools.partial(gather_kernel, n_seq, n_dp),
        out_shape=(
            jax.ShapeDtypeStruct((n_seq,) + halves.shape, bf16),
            jax.ShapeDtypeStruct((n_dp,) + pieces.shape, bf16),
        ),
        in_specs=[pl.BlockSpec(memory_space=pl.ANY)] * 2,
        out_specs=(pl.BlockSpec(memory_space=pl.ANY),) * 2,
        scratch_shapes=[
            pltpu.SemaphoreType.DMA((2 * n_a + 2 * (n_a - 1),)),
            pltpu.SemaphoreType.DMA((n_seq, 2)),
            pltpu.SemaphoreType.DMA((4 * n_c * 2,)),
            pltpu.SemaphoreType.DMA((n_dp, 2)),
            pltpu.SemaphoreType.DMA((2,)),
        ],
        compiler_params=pltpu.CompilerParams(collective_id=0, has_side_effects=True),
        name="gather_both",
    )(halves, pieces)
    return f_all.reshape(n_seq * clips * slab_len, width), w_all.reshape(n_dp * depth, columns)


def exchange_kernel(n_seq, source, result, send, recv, own_sem):
    me = lax.axis_index("seq")
    own = pltpu.make_async_copy(source.at[me], result.at[me], own_sem.at[0])
    own.start()
    barrier = pltpu.get_barrier_semaphore()
    others = [lax.rem(me + i, n_seq) for i in range(1, n_seq)]
    for other in others:
        pl.semaphore_signal(
            barrier, inc=1, device_id={"seq": other}, device_id_type=pl.DeviceIdType.MESH
        )
    pl.semaphore_wait(barrier, n_seq - 1)
    copies = []
    for i, other in enumerate(others):
        copy = pltpu.make_async_remote_copy(
            source.at[other],
            result.at[me],
            send.at[i],
            recv.at[me],
            device_id={"seq": other},
            device_id_type=pl.DeviceIdType.MESH,
        )
        copy.start()
        copies.append(copy)
    for other in others:
        pltpu.make_async_remote_copy(
            source.at[other],
            result.at[other],
            send.at[0],
            recv.at[other],
            device_id={"seq": other},
            device_id_type=pl.DeviceIdType.MESH,
        ).wait_recv()
    for copy in copies:
        copy.wait_send()
    own.wait()


def exchange(blocks, n_seq):
    return pl.pallas_call(
        functools.partial(exchange_kernel, n_seq),
        out_shape=jax.ShapeDtypeStruct(blocks.shape, blocks.dtype),
        in_specs=[pl.BlockSpec(memory_space=pl.ANY)],
        out_specs=pl.BlockSpec(memory_space=pl.ANY),
        scratch_shapes=[
            pltpu.SemaphoreType.DMA((n_seq - 1,)),
            pltpu.SemaphoreType.DMA((n_seq,)),
            pltpu.SemaphoreType.DMA((1,)),
        ],
        compiler_params=pltpu.CompilerParams(collective_id=1, has_side_effects=True),
        name="exchange",
    )(blocks)


def on_device(
    frames,
    proj_weight,
    rate_weight,
    rate_bias,
    init_weights,
    init_bias_hidden,
    init_bias_out,
    out_gain,
):
    clips, slab_len, model_width = frames.shape
    heads = rate_weight.shape[1]
    size = init_weights.shape[2]
    inner = init_weights.shape[3]
    length = lax.axis_size("seq")
    position = lax.axis_index("seq")
    mine = heads // length
    groups = -(-mine // PAIR)
    padded = groups * PAIR
    lanes = PAIR * size
    blocks = clips * PAIR
    batches = slab_len // MB
    first = position * mine

    def own(array, axis):
        part = lax.dynamic_slice_in_dim(array, first, mine, axis)
        pads = [(0, 0)] * array.ndim
        pads[axis] = (0, padded - mine)
        return jnp.pad(part, pads) if padded > mine else part

    span = proj_weight.shape[1] // 3
    parts = [
        lax.dynamic_slice_in_dim(proj_weight, part * span + first * size, mine * size, 1)
        for part in range(3)
    ]
    if padded > mine:
        parts = [jnp.pad(part, ((0, 0), (0, (padded - mine) * size))) for part in parts]
    weight = jnp.concatenate(parts, axis=1)
    rows, weight = gather_both(frames, weight, length, lax.axis_size("dp"))
    projected = jnp.dot(rows, weight, preferred_element_type=f32).astype(bf16)
    projected = projected.reshape(length, clips, slab_len, groups * 3 * lanes)
    rates = jnp.dot(rows, own(rate_weight, 1), preferred_element_type=f32)
    rates = jax.nn.sigmoid(rates + own(rate_bias, 0)) / (MB * (size + inner))
    rates = rates.reshape(length, clips, batches, MB, groups, PAIR).transpose(4, 0, 2, 1, 5, 3)
    rates = rates.reshape(groups, length * batches, 1, blocks * MB)
    w_own = own(init_weights, 1).reshape(2, groups, lanes, inner)
    b1 = own(init_bias_hidden, 0).reshape(groups, 1, PAIR, inner)
    b1 = jnp.broadcast_to(b1, (groups, clips, PAIR, inner)).reshape(groups, blocks, inner)
    b1 = jnp.pad(b1, ((0, 0), (0, 8 - blocks), (0, 0)))
    b2 = own(init_bias_out, 0).reshape(groups, 1, 1, lanes)
    b2 = jnp.broadcast_to(b2, (groups, 8, clips, lanes)).reshape(groups, 8, blocks * size)
    gain = own(out_gain.reshape(heads, size), 0).reshape(groups, 1, 1, lanes)
    gain = jnp.broadcast_to(gain, (groups, 1, clips, lanes)).reshape(groups, 1, blocks * size)

    results = pl.pallas_call(
        functools.partial(ttt_kernel, groups, clips),
        out_shape=jax.ShapeDtypeStruct((length, clips, slab_len, groups * lanes), bf16),
        in_specs=[pl.BlockSpec(memory_space=pltpu.VMEM)] * 7,
        out_specs=pl.BlockSpec(memory_space=pltpu.VMEM),
        scratch_shapes=[
            pltpu.VMEM((blocks * size, inner), f32),
            pltpu.VMEM((8, inner), f32),
            pltpu.VMEM((blocks * size, inner), f32),
            pltpu.VMEM((8, blocks * size), f32),
        ]
        * groups,
        compiler_params=pltpu.CompilerParams(vmem_limit_bytes=48 * 1024 * 1024),
        name="fast_state",
    )(projected, rates, w_own[0], b1, w_own[1], b2, gain)

    exchanged = exchange(results, length)
    exchanged = exchanged[..., : mine * size]
    return exchanged.transpose(1, 2, 0, 3).reshape(clips, slab_len, heads * size)


def solution(mesh):
    return jax.shard_map(
        on_device,
        mesh=mesh,
        in_specs=(P("dp", "seq", None), P("dp", None), P(), P(), P(), P(), P(), P()),
        out_specs=P("dp", "seq", None),
        check_vma=False,
    )
```

```python
import functools
import math

import jax
import jax.numpy as jnp
from jax import lax
from jax.experimental import pallas as pl
from jax.experimental.pallas import tpu as pltpu
from jax.sharding import PartitionSpec as P

MB = 64
PAIR = 2
coefficient = 0.044715
root_scale = math.sqrt(2.0 / math.pi)
f32 = jnp.float32
bf16 = jnp.bfloat16


def gelu_value(z):
    u = z * z
    t = jnp.tanh(z * (root_scale + (root_scale * coefficient) * u))
    h = 0.5 * z
    return h + h * t


def gelu_pair(z):
    u = z * z
    t = jnp.tanh(z * (root_scale + (root_scale * coefficient) * u))
    h = 0.5 * z
    value = h + h * t
    slope = (0.5 + 0.5 * t) + h * (1.0 - t * t) * (
        root_scale + (3.0 * root_scale * coefficient) * u
    )
    return value, slope


def dot(a, b):
    return jnp.dot(a, b, preferred_element_type=f32)


def dot_t(a, b):
    return lax.dot_general(a, b, (((1,), (1,)), ((), ())), preferred_element_type=f32)


def block_masks(width, step):
    rows = lax.broadcasted_iota(jnp.int32, (width, width), 0)
    cols = lax.broadcasted_iota(jnp.int32, (width, width), 1)
    same = (rows // step) == (cols // step)
    return same, same & (cols <= rows)


def ttt_step(read, state, rate_row, gain_row, masks, blocks):
    same, causal = masks
    w1_ref, b1_ref, w2_ref, b2_ref = state
    step = MB
    width = blocks * step
    q, k, v = read
    zero = jnp.zeros((), bf16)
    k_bd = jnp.where(same, jnp.concatenate([k] * blocks, axis=0), zero)
    q_bd = jnp.where(same, jnp.concatenate([q] * blocks, axis=0), zero)
    w1 = w1_ref[...]
    w2 = w2_ref[...]
    w1_low = w1.astype(bf16)
    w2_low = w2.astype(bf16)
    b1 = b1_ref[...]
    b2 = b2_ref[0:1, :]
    b1_rows = jnp.concatenate(
        [jnp.broadcast_to(b1[i : i + 1], (step, b1.shape[1])) for i in range(blocks)], axis=0
    )
    z1 = dot(k_bd, w1_low) + b1_rows
    x2, slope = gelu_pair(z1)
    x2_low = x2.astype(bf16)
    target = b2 - (v.astype(f32) - k.astype(f32))
    z2 = dot_t(x2_low, w2_low)
    g2 = jnp.where(same, z2 + jnp.concatenate([target] * blocks, axis=0), 0.0)
    g2_low = g2.astype(bf16)
    g1_low = (dot(g2_low, w2_low) * slope).astype(bf16)
    m1 = jnp.where(causal, (dot_t(q_bd, k_bd) + 1.0) * rate_row, 0.0).astype(bf16)
    z1q = dot(q_bd, w1_low) + b1_rows - dot(m1, g1_low)
    x2q_low = gelu_value(z1q).astype(bf16)
    m2 = jnp.where(causal, (dot_t(x2q_low, x2_low) + 1.0) * rate_row, 0.0).astype(bf16)
    z2q = dot_t(x2q_low, w2_low) - dot(m2, g2_low)
    lane = lax.broadcasted_iota(jnp.int32, (step, width), 1) // step
    out = z2q[:step]
    for i in range(1, blocks):
        out = jnp.where(lane == i, z2q[i * step : (i + 1) * step], out)
    y = q.astype(f32) + out + b2
    member = lax.broadcasted_iota(jnp.int32, (8, width), 0)
    rate_bd = jnp.where(
        member == lax.broadcasted_iota(jnp.int32, (8, width), 1) // step, rate_row, 0.0
    ).astype(bf16)
    k_scaled = (k_bd.astype(f32).T * rate_row).astype(bf16)
    g2_scaled = (g2.T * rate_row).astype(bf16)
    w1_ref[...] = w1 - dot(k_scaled, g1_low)
    b1_ref[...] = b1 - dot(rate_bd, g1_low)
    w2_ref[...] = w2 - dot(g2_scaled, x2_low)
    db2 = dot(rate_bd, g2_low)
    b2_ref[0:1, :] = b2 - jnp.sum(db2, axis=0, keepdims=True)
    square = dot((y * y).astype(bf16), same.astype(bf16)) * (1.0 / step)
    return y * lax.rsqrt(square + 1e-06) * gain_row


def round_state(state):
    for ref in state:
        ref[...] = ref[...].astype(bf16).astype(f32)


def ttt_kernel(groups, clips, proj_ref, rate_ref, w1_in, b1_in, w2_in, b2_in, gain_ref, out_ref, *scratch):
    blocks = clips * PAIR
    slabs = proj_ref.shape[0]
    batches = proj_ref.shape[2] // MB
    lanes = PAIR * MB
    states = [scratch[4 * g : 4 * g + 4] for g in range(groups)]
    for g in range(groups):
        for c in range(clips):
            states[g][0][c * lanes : (c + 1) * lanes, :] = w1_in[g]
            states[g][2][c * lanes : (c + 1) * lanes, :] = w2_in[g]
        states[g][1][...] = b1_in[g]
        states[g][3][...] = b2_in[g]

    def slab_body(s, carry):
        masks = block_masks(blocks * MB, MB)
        for b in range(batches):
            for g in range(groups):
                read = [
                    jnp.concatenate(
                        [
                            proj_ref[s, c, b * MB : (b + 1) * MB, (part * groups + g) * lanes : (part * groups + g + 1) * lanes]
                            for c in range(clips)
                        ],
                        axis=1,
                    )
                    for part in range(3)
                ]
                y = ttt_step(
                    read, states[g], rate_ref[g, s * batches + b], gain_ref[g], masks, blocks
                ).astype(bf16)
                for c in range(clips):
                    out_ref[s, c, b * MB : (b + 1) * MB, g * lanes : (g + 1) * lanes] = y[
                        :, c * lanes : (c + 1) * lanes
                    ]
        for g in range(groups):
            round_state(states[g])
        return carry

    lax.fori_loop(0, slabs, slab_body, 0)


def gather_kernel(
    n_seq, n_dp, f_ref, w_ref, r_ref, proj_out, logit_out,
    f_all, w_all, acc, f_send, f_recv, w_send, w_recv, own_sem
):
    rows = 2 * f_ref.shape[1]
    width = f_ref.shape[2]
    columns = w_ref.shape[2]
    chip_depth = 2 * 2 * w_ref.shape[1]
    seq, dp = lax.axis_index("seq"), lax.axis_index("dp")
    a, b = seq // 2, lax.rem(seq, 2)
    z, c = dp // 2, lax.rem(dp, 2)
    n_a, n_c = n_seq // 2, n_dp // 2
    peers = [lax.rem(a + i, n_a) * 2 + b for i in range(1, n_a)]
    pair = a * 2 + 1 - b
    sibling = z * 2 + 1 - c
    has_right, has_left = z + 1 < n_c, z > 0

    own_f = pltpu.make_async_copy(f_ref, f_all.at[seq], own_sem.at[0])
    own_w = pltpu.make_async_copy(w_ref, w_all.at[dp], own_sem.at[1])
    own_f.start()
    own_w.start()

    def zero_body(s, carry):
        acc[s] = jnp.zeros(acc.shape[1:], f32)
        return carry

    lax.fori_loop(0, n_seq, zero_body, 0)

    barrier = pltpu.get_barrier_semaphore()
    for other in peers + [pair]:
        pl.semaphore_signal(
            barrier, inc=1, device_id={"seq": other}, device_id_type=pl.DeviceIdType.MESH
        )
    pl.semaphore_signal(
        barrier, inc=1, device_id={"dp": sibling}, device_id_type=pl.DeviceIdType.MESH
    )

    @pl.when(has_right)
    def _():
        pl.semaphore_signal(
            barrier, inc=1, device_id={"dp": dp + 2}, device_id_type=pl.DeviceIdType.MESH
        )

    @pl.when(has_left)
    def _():
        pl.semaphore_signal(
            barrier, inc=1, device_id={"dp": dp - 2}, device_id_type=pl.DeviceIdType.MESH
        )

    neighbours = jnp.where(has_right, 1, 0) + jnp.where(has_left, 1, 0)
    pl.semaphore_wait(barrier, neighbours + (len(peers) + 2))

    pending = []

    def send_f(source, owner, half, to):
        copy = pltpu.make_async_remote_copy(
            source,
            f_all.at[owner, half],
            f_send.at[len(pending)],
            f_recv.at[owner, half],
            device_id={"seq": to},
            device_id_type=pl.DeviceIdType.MESH,
        )
        copy.start()
        pending.append(copy)

    def got_f(owner, half):
        pltpu.make_async_remote_copy(
            f_all.at[owner, half],
            f_all.at[owner, half],
            f_send.at[0],
            f_recv.at[owner, half],
            device_id={"seq": pair},
            device_id_type=pl.DeviceIdType.MESH,
        ).wait_recv()

    def copy_w(source, owner, piece, way, distance):
        to = (dp + 2, dp - 2, sibling)[way]
        return pltpu.make_async_remote_copy(
            source,
            w_all.at[owner, piece],
            w_send.at[(way * n_c + distance) * 2 + piece],
            w_recv.at[owner, piece],
            device_id={"dp": to},
            device_id_type=pl.DeviceIdType.MESH,
        )

    def got_w(owner, piece):
        copy_w(w_all.at[owner, piece], owner, piece, 2, 0).wait_recv()

    for piece in range(2):

        @pl.when(has_right)
        def _():
            copy_w(w_ref.at[piece], dp, piece, 0, 0).start()

        @pl.when(has_left)
        def _():
            copy_w(w_ref.at[piece], dp, piece, 1, 0).start()

    for half in (0, 1):
        for other in peers:
            send_f(f_ref.at[half], seq, half, other)
        send_f(f_ref.at[1 - half], seq, 1 - half, pair)
    for piece in range(2):
        copy_w(w_ref.at[piece], dp, piece, 2, 0).start()

    def pass_on(distance):
        for piece in range(2):
            for way, sign, here, onward in (
                (0, -1, z >= distance, has_right),
                (1, 1, z + distance < n_c, has_left),
            ):
                owner = dp + sign * 2 * distance

                @pl.when(here)
                def _():
                    got_w(owner, piece)

                    if distance < n_c - 1:

                        @pl.when(onward)
                        def _():
                            copy_w(w_all.at[owner, piece], owner, piece, way, distance).start()

                    share(w_all, w_send, w_recv, owner, piece, way, distance, n_c, sibling).start()

    def sibling_rows(chip):
        for piece in range(2):
            got_w(chip * 2 + 1 - c, piece)

    def add_product(chip):
        def body(s, carry):
            left = f_all[s].reshape(rows, width)[:, chip * chip_depth : (chip + 1) * chip_depth]
            right = w_all[2 * chip : 2 * chip + 2].reshape(chip_depth, columns)
            acc[s] = acc[s] + dot(left, right)
            return carry

        lax.fori_loop(0, n_seq, body, 0)

    for distance in range(1, n_c - 1):
        pass_on(distance)
        if distance == 1:
            relay_f(peers, pair, got_f, send_f, f_all)
    if n_c <= 2:
        relay_f(peers, pair, got_f, send_f, f_all)

    for other in peers:
        got_f(other, 1)
        far = other + 1 - 2 * b
        got_f(far, 0)
        got_f(far, 1)
    got_f(pair, 0)
    own_f.wait()
    own_w.wait()

    def rate_body(s, carry):
        logit_out[s] = dot(f_all[s].reshape(rows, width), r_ref[...])
        return carry

    lax.fori_loop(0, n_seq, rate_body, 0)
    aligned = chip_depth % 128 == 0
    ends = (0, n_c - 1) if n_c > 1 else ()
    if aligned:
        for chip in range(n_c):
            if chip in ends:

                @pl.when(z != n_c - 1 - chip)
                def _():
                    sibling_rows(chip)
                    add_product(chip)
            else:
                sibling_rows(chip)
                add_product(chip)
        if n_c > 1:
            pass_on(n_c - 1)
        for chip in ends:

            @pl.when(z == n_c - 1 - chip)
            def _():
                sibling_rows(chip)
                add_product(chip)
    else:
        if n_c > 1:
            pass_on(n_c - 1)
        for chip in range(n_c):
            sibling_rows(chip)

        def whole_body(s, carry):
            left = f_all[s].reshape(rows, width)
            acc[s] = acc[s] + dot(left, w_all[...].reshape(width, columns))
            return carry

        lax.fori_loop(0, n_seq, whole_body, 0)

    def round_body(s, carry):
        proj_out[s] = acc[s].astype(bf16)
        return carry

    lax.fori_loop(0, n_seq, round_body, 0)

    for copy in pending:
        copy.wait_send()
    for piece in range(2):

        @pl.when(has_right)
        def _():
            copy_w(w_ref.at[piece], dp, piece, 0, 0).wait_send()

        @pl.when(has_left)
        def _():
            copy_w(w_ref.at[piece], dp, piece, 1, 0).wait_send()

        copy_w(w_ref.at[piece], dp, piece, 2, 0).wait_send()
        for distance in range(1, n_c):
            for way, sign, here, onward in (
                (0, -1, z >= distance, has_right),
                (1, 1, z + distance < n_c, has_left),
            ):
                owner = dp + sign * 2 * distance

                @pl.when(here)
                def _():
                    if distance < n_c - 1:

                        @pl.when(onward)
                        def _():
                            copy_w(w_all.at[owner, piece], owner, piece, way, distance).wait_send()

                    share(
                        w_all, w_send, w_recv, owner, piece, way, distance, n_c, sibling
                    ).wait_send()


def relay_f(peers, pair, got_f, send_f, f_all):
    for other in peers:
        got_f(other, 0)
        send_f(f_all.at[other, 0], other, 0, pair)
    got_f(pair, 1)
    for other in peers:
        send_f(f_all.at[pair, 1], pair, 1, other)


def share(w_all, w_send, w_recv, owner, piece, way, distance, n_c, sibling):
    return pltpu.make_async_remote_copy(
        w_all.at[owner, piece],
        w_all.at[owner, piece],
        w_send.at[((2 + way) * n_c + distance) * 2 + piece],
        w_recv.at[owner, piece],
        device_id={"dp": sibling},
        device_id_type=pl.DeviceIdType.MESH,
    )


def gather_project(frames, weight, rate_columns, n_seq, n_dp):
    clips, slab_len, width = frames.shape
    depth, columns = weight.shape
    n_a, n_c = n_seq // 2, n_dp // 2
    rows = clips * slab_len
    halves = frames.reshape(2, rows // 2, width)
    pieces = weight.reshape(2, depth // 2, columns)
    return pl.pallas_call(
        functools.partial(gather_kernel, n_seq, n_dp),
        out_shape=(
            jax.ShapeDtypeStruct((n_seq, rows, columns), bf16),
            jax.ShapeDtypeStruct((n_seq, rows, rate_columns.shape[1]), f32),
        ),
        in_specs=[
            pl.BlockSpec(memory_space=pl.ANY),
            pl.BlockSpec(memory_space=pl.ANY),
            pl.BlockSpec(memory_space=pltpu.VMEM),
        ],
        out_specs=(pl.BlockSpec(memory_space=pltpu.VMEM),) * 2,
        scratch_shapes=[
            pltpu.VMEM((n_seq,) + halves.shape, bf16),
            pltpu.VMEM((n_dp,) + pieces.shape, bf16),
            pltpu.VMEM((n_seq, rows, columns), f32),
            pltpu.SemaphoreType.DMA((2 * n_a + 2 * (n_a - 1),)),
            pltpu.SemaphoreType.DMA((n_seq, 2)),
            pltpu.SemaphoreType.DMA((4 * n_c * 2,)),
            pltpu.SemaphoreType.DMA((n_dp, 2)),
            pltpu.SemaphoreType.DMA((2,)),
        ],
        compiler_params=pltpu.CompilerParams(
            collective_id=0, has_side_effects=True, vmem_limit_bytes=48 * 1024 * 1024
        ),
        name="gather_project",
    )(halves, pieces, rate_columns)


def exchange_kernel(n_seq, source, result, send, recv, own_sem):
    me = lax.axis_index("seq")
    own = pltpu.make_async_copy(source.at[me], result.at[me], own_sem.at[0])
    own.start()
    barrier = pltpu.get_barrier_semaphore()
    others = [lax.rem(me + i, n_seq) for i in range(1, n_seq)]
    for other in others:
        pl.semaphore_signal(
            barrier, inc=1, device_id={"seq": other}, device_id_type=pl.DeviceIdType.MESH
        )
    pl.semaphore_wait(barrier, n_seq - 1)
    copies = []
    for i, other in enumerate(others):
        copy = pltpu.make_async_remote_copy(
            source.at[other],
            result.at[me],
            send.at[i],
            recv.at[me],
            device_id={"seq": other},
            device_id_type=pl.DeviceIdType.MESH,
        )
        copy.start()
        copies.append(copy)
    for other in others:
        pltpu.make_async_remote_copy(
            source.at[other],
            result.at[other],
            send.at[0],
            recv.at[other],
            device_id={"seq": other},
            device_id_type=pl.DeviceIdType.MESH,
        ).wait_recv()
    for copy in copies:
        copy.wait_send()
    own.wait()


def exchange(blocks, n_seq):
    return pl.pallas_call(
        functools.partial(exchange_kernel, n_seq),
        out_shape=jax.ShapeDtypeStruct(blocks.shape, blocks.dtype),
        in_specs=[pl.BlockSpec(memory_space=pl.ANY)],
        out_specs=pl.BlockSpec(memory_space=pl.ANY),
        scratch_shapes=[
            pltpu.SemaphoreType.DMA((n_seq - 1,)),
            pltpu.SemaphoreType.DMA((n_seq,)),
            pltpu.SemaphoreType.DMA((1,)),
        ],
        compiler_params=pltpu.CompilerParams(collective_id=1, has_side_effects=True),
        name="exchange",
    )(blocks)


def on_device(
    frames,
    proj_weight,
    rate_weight,
    rate_bias,
    init_weights,
    init_bias_hidden,
    init_bias_out,
    out_gain,
):
    clips, slab_len, model_width = frames.shape
    heads = rate_weight.shape[1]
    size = init_weights.shape[2]
    inner = init_weights.shape[3]
    length = lax.axis_size("seq")
    position = lax.axis_index("seq")
    mine = heads // length
    groups = -(-mine // PAIR)
    padded = groups * PAIR
    lanes = PAIR * size
    blocks = clips * PAIR
    batches = slab_len // MB
    first = position * mine

    def own(array, axis):
        part = lax.dynamic_slice_in_dim(array, first, mine, axis)
        pads = [(0, 0)] * array.ndim
        pads[axis] = (0, padded - mine)
        return jnp.pad(part, pads) if padded > mine else part

    span = proj_weight.shape[1] // 3
    parts = [
        lax.dynamic_slice_in_dim(proj_weight, part * span + first * size, mine * size, 1)
        for part in range(3)
    ]
    if padded > mine:
        parts = [jnp.pad(part, ((0, 0), (0, (padded - mine) * size))) for part in parts]
    weight = jnp.concatenate(parts, axis=1)
    rate_columns = jnp.pad(own(rate_weight, 1), ((0, 0), (0, 128 - padded)))
    projected, logits = gather_project(
        frames, weight, rate_columns, length, lax.axis_size("dp")
    )
    projected = projected.reshape(length, clips, slab_len, groups * 3 * lanes)
    rates = logits[..., :padded]
    rates = jax.nn.sigmoid(rates + own(rate_bias, 0)) / (MB * (size + inner))
    rates = rates.reshape(length, clips, batches, MB, groups, PAIR).transpose(4, 0, 2, 1, 5, 3)
    rates = rates.reshape(groups, length * batches, 1, blocks * MB)
    w_own = own(init_weights, 1).reshape(2, groups, lanes, inner)
    b1 = own(init_bias_hidden, 0).reshape(groups, 1, PAIR, inner)
    b1 = jnp.broadcast_to(b1, (groups, clips, PAIR, inner)).reshape(groups, blocks, inner)
    b1 = jnp.pad(b1, ((0, 0), (0, 8 - blocks), (0, 0)))
    b2 = own(init_bias_out, 0).reshape(groups, 1, 1, lanes)
    b2 = jnp.broadcast_to(b2, (groups, 8, clips, lanes)).reshape(groups, 8, blocks * size)
    gain = own(out_gain.reshape(heads, size), 0).reshape(groups, 1, 1, lanes)
    gain = jnp.broadcast_to(gain, (groups, 1, clips, lanes)).reshape(groups, 1, blocks * size)

    results = pl.pallas_call(
        functools.partial(ttt_kernel, groups, clips),
        out_shape=jax.ShapeDtypeStruct((length, clips, slab_len, groups * lanes), bf16),
        in_specs=[pl.BlockSpec(memory_space=pltpu.VMEM)] * 7,
        out_specs=pl.BlockSpec(memory_space=pltpu.VMEM),
        scratch_shapes=[
            pltpu.VMEM((blocks * size, inner), f32),
            pltpu.VMEM((8, inner), f32),
            pltpu.VMEM((blocks * size, inner), f32),
            pltpu.VMEM((8, blocks * size), f32),
        ]
        * groups,
        compiler_params=pltpu.CompilerParams(vmem_limit_bytes=48 * 1024 * 1024),
        name="fast_state",
    )(projected, rates, w_own[0], b1, w_own[1], b2, gain)

    exchanged = exchange(results, length)
    exchanged = exchanged[..., : mine * size]
    return exchanged.transpose(1, 2, 0, 3).reshape(clips, slab_len, heads * size)


def solution(mesh):
    return jax.shard_map(
        on_device,
        mesh=mesh,
        in_specs=(P("dp", "seq", None), P("dp", None), P(), P(), P(), P(), P(), P()),
        out_specs=P("dp", "seq", None),
        check_vma=False,
    )
```
